32 devices in a mesh: ang: 8 (over y, x, core), kslab: 4 (over z).
Axes of the slice: x: 2, y: 2, z: 4, core: 2. Of those that a mesh axis runs over, the one named last changes fastest.
Arguments:
- amplitude: bfloat16 [256, 112, 8, 2048], P('ang', None, 'kslab'), may hold values from -6 to 6
- ps_form: bfloat16 [2048, 896], replicated, may hold values from -0.125 to 0.125
- kgrid: float32 [8], replicated, may hold values from 0.1 to 3
- l_atom: int32 [112], replicated, may hold values from 0 to 7
- l_ps: int32 [112], replicated, may hold values from 0 to 7
- sixj: float32 [4, 12, 8, 8], replicated, may hold values from -0.5 to 0.5
Outputs:
- kernel: float32 [112, 4, 8, 896], P('ang', 'kslab')
The draws below stay inside these ranges and needn't reach their ends.
All inputs are finite; a program needn't handle non-finite values.
Results may differ from the reference program's by a relative error of at most 0.0003.
Values sent between devices are 32-bit elements; how exact they have to be, the bound alone decides.
A program may use at most 128 MiB of HBM per device.

```python
import math
import jax
import jax.numpy as jnp
from jax import lax

NG = 256
NL = 12
NK = 8
M = 2048
LCH = 8
PS_CH = 112
ATOM_CH = 112
NJ = 4
COLS = 896


def touch_ends(array, stream_key, least, high):
    spot = [jax.random.randint(jax.random.fold_in(stream_key, axis), (), 0, length) for axis, length in enumerate(array.shape)]
    main_axis = array.shape.index(max(array.shape))
    next_to = spot[:main_axis] + [(spot[main_axis] + 1) % array.shape[main_axis]] + spot[main_axis + 1:]
    return array.at[tuple(spot)].set(least).at[tuple(next_to)].set(high)


def level_of(stream_key, dims, pieces, least, high):
    level, own = 1.0, jax.random.fold_in(stream_key, 6)
    for position, parts in pieces:
        draws = jnp.exp(jax.random.uniform(jax.random.fold_in(own, position), (parts,), jnp.float32, least / len(pieces), high / len(pieces)))
        level = level * jnp.repeat(draws, dims[position] // parts).reshape([-1 if axis == position else 1 for axis in range(len(dims))])
    return level


def noise(stream_key, extent, scale, most, split=(), kind=jnp.bfloat16):
    level = level_of(stream_key, extent, split, -0.22, 0.18) if split else 1.0
    drawn = jax.random.normal(stream_key, extent, jnp.float32) * scale * level
    return jnp.minimum(jnp.maximum(drawn, -most), most).astype(kind)


def setup_inputs(seed: int = 0) -> dict:
    seeds = jax.random.split(jax.random.key(seed), 7)
    return {
        "amplitude": noise(seeds[0], (NG, ATOM_CH, NK, M), 1.0, 6.0, ((0, 8), (2, 4))),
        "ps_form": noise(seeds[1], (M, COLS), M ** -0.5, 0.125),
        "kgrid": jnp.clip(jnp.exp(jax.random.uniform(seeds[2], (NK,), jnp.float32, math.log(0.1), math.log(3.0))), 0.1, 3.0),
        "l_atom": touch_ends(jax.random.randint(seeds[3], (ATOM_CH,), 0, LCH), jax.random.fold_in(seeds[3], 1), 0, LCH - 1).astype(jnp.int32),
        "l_ps": touch_ends(jax.random.randint(seeds[4], (PS_CH,), 0, LCH), jax.random.fold_in(seeds[4], 1), 0, LCH - 1).astype(jnp.int32),
        "sixj": jnp.clip(jax.random.uniform(seeds[5], (NJ, NL, LCH, LCH), jnp.float32, -0.5, 0.5), -0.5, 0.5),
    }


def legendre_table(first_row, row_count, total_points, degrees):
    positions = (first_row + jnp.arange(row_count)).astype(jnp.float32)
    angles = jnp.pi * (positions + 0.5) / total_points
    grid_nodes = jnp.cos(angles)
    grid_weights = (jnp.pi / total_points) * jnp.sin(angles)
    series = [jnp.ones_like(grid_nodes), grid_nodes]
    for degree in range(1, degrees - 1):
        series.append(((2 * degree + 1) * grid_nodes * series[-1] - degree * series[-2]) / (degree + 1))
    return grid_nodes, grid_weights[None, :] * jnp.stack(series[:degrees])


def reference(amplitude, ps_form, kgrid, l_atom, l_ps, sixj):
    grid_nodes, projector = legendre_table(0, NG, NG, NL)
    kcolumn = jnp.tile(kgrid, PS_CH)
    krow = kgrid[None, :, None]
    kcol = kcolumn[None, None, :]
    qinverse = 1.0 / (1.0 + krow * krow + kcol * kcol - 2.0 * grid_nodes[:, None, None] * krow * kcol)
    levels = jnp.arange(LCH, dtype=jnp.int32)
    onehot_ps = (l_ps[:, None] == levels[None, :]).astype(jnp.float32)

    def channel_kernel(channel):
        slab_data = lax.dynamic_index_in_dim(amplitude, channel, 1, keepdims=False)
        intersection = jnp.dot(slab_data.reshape(-1, M), ps_form, preferred_element_type=jnp.float32)
        intersection = intersection.reshape(NG, NK, COLS)
        values = jnp.einsum("lg,gkc->lkc", projector, intersection * qinverse, precision=lax.Precision.HIGHEST)
        atom_level = lax.dynamic_index_in_dim(l_atom, channel, 0, keepdims=False)
        onehot_atom = (levels == atom_level).astype(jnp.float32)
        coupling = jnp.einsum("jlxy,x,by->jlb", sixj, onehot_atom, onehot_ps, precision=lax.Precision.HIGHEST)
        widened = jnp.repeat(coupling, NK, axis=2)
        return jnp.einsum("jlc,lkc->jkc", widened, values, precision=lax.Precision.HIGHEST)

    return lax.map(channel_kernel, jnp.arange(ATOM_CH, dtype=jnp.int32))
```

```python
import functools

import jax
import jax.numpy as jnp
from jax import lax
from jax.experimental import pallas as pl
from jax.experimental.pallas import tpu as pltpu
from jax.sharding import PartitionSpec as P


def legendre_table(first_row, row_count, total_points, degrees):
    positions = (first_row + jnp.arange(row_count)).astype(jnp.float32)
    angles = jnp.pi * (positions + 0.5) / total_points
    grid_nodes = jnp.cos(angles)
    grid_weights = jnp.pi / total_points * jnp.sin(angles)
    series = [jnp.ones_like(grid_nodes), grid_nodes]
    for degree in range(1, degrees - 1):
        series.append(
            ((2 * degree + 1) * grid_nodes * series[-1] - degree * series[-2]) / (degree + 1)
        )
    return (grid_nodes, grid_weights[None, :] * jnp.stack(series[:degrees]))


def recouple(values, l_atom, l_ps, sixj, kpoints):
    levels = jnp.arange(sixj.shape[2], dtype=jnp.int32)
    onehot_atom = (l_atom[:, None] == levels[None, :]).astype(jnp.float32)
    onehot_ps = (l_ps[:, None] == levels[None, :]).astype(jnp.float32)
    coupling = jnp.einsum(
        "jlxy,ax,by->ajlb", sixj, onehot_atom, onehot_ps, precision=lax.Precision.HIGHEST
    )
    widened = jnp.repeat(coupling, kpoints, axis=3)
    return jnp.einsum("ajlc,alkc->ajkc", widened, values, precision=lax.Precision.HIGHEST)


def plain(amplitude, ps_form, kgrid, l_atom, l_ps, sixj):
    grid_count, channels, slab_points, radial = amplitude.shape
    columns = ps_form.shape[1]
    kpoints = kgrid.shape[0]
    ps_channels = columns // kpoints
    degrees = sixj.shape[1]
    ang_size = lax.axis_size("ang")
    owned = channels // ang_size
    grid_nodes, projector = legendre_table(
        lax.axis_index("ang") * grid_count, grid_count, grid_count * ang_size, degrees
    )
    krow = lax.dynamic_slice_in_dim(kgrid, lax.axis_index("kslab") * slab_points, slab_points)[
        None, :, None
    ]
    kcol = jnp.tile(kgrid, ps_channels)[None, None, :]
    qinverse = 1.0 / (
        1.0 + krow * krow + kcol * kcol - 2.0 * grid_nodes[:, None, None] * krow * kcol
    )
    intersection = jnp.dot(
        amplitude.reshape(-1, radial), ps_form, preferred_element_type=jnp.float32
    )
    intersection = intersection.reshape(
        grid_count, lax.axis_size("ang") * owned, slab_points, columns
    )
    integrand = intersection * qinverse[:, None]
    partial = jnp.einsum("lg,gakc->alkc", projector, integrand, precision=lax.Precision.HIGHEST)
    partial = recouple(partial, l_atom, l_ps, sixj, kpoints)
    summed = lax.psum_scatter(partial, "ang", scatter_dimension=0, tiled=True)
    return lax.all_to_all(summed, "kslab", split_axis=1, concat_axis=2, tiled=True)


LANES = 128


def column_chunks(columns):
    width = 2 * LANES
    return [(first, min(width, columns - first)) for first in range(0, columns, width)]


def weigh(acc, weights, levels, partial, first_atom, chunk, sizes):
    grid_count, owned, slab_points, total_j = sizes
    first, width = chunk
    group = owned * slab_points
    for atom in range(owned):
        level = levels[first_atom + atom]
        for tile in range(width // LANES):
            lanes = pl.ds(first + tile * LANES, LANES)
            points = [
                acc[tile, pl.ds(atom * slab_points + k, grid_count, stride=group), :]
                for k in range(slab_points)
            ]
            rows = []
            for j in range(total_j):
                for k in range(slab_points):
                    term = points[k] * weights[level, j * slab_points + k, :, lanes]
                    rows.append(jnp.sum(term, axis=0, keepdims=True))
            partial[atom, :, lanes] = jnp.concatenate(rows, axis=0)


def fetch(amplitude, slab, sems, slot, first_atom, owned):
    return [
        pltpu.make_async_copy(
            amplitude.at[:, pl.ds(first_atom, owned), :, pl.ds(piece * LANES, LANES)],
            slab.at[slot, piece],
            sems.at[slot, piece],
        )
        for piece in range(slab.shape[1])
    ]


def block_kernel(sizes, amplitude, ps_form, weights, levels, partial, slab, acc_a, acc_b, sems):
    grid_count, owned, slab_points, total_j = sizes
    pieces = slab.shape[1]
    rows = grid_count * owned * slab_points
    blocks = partial.shape[0] // owned
    chunks = column_chunks(ps_form.shape[1])
    accs = (acc_a, acc_b)
    for copy in fetch(amplitude, slab, sems, 0, 0, owned):
        copy.start()

    def step(block, carry):
        slot = lax.rem(block, 2)
        first_atom = block * owned
        for copy in fetch(amplitude, slab, sems, slot, first_atom, owned):
            copy.wait()

        @pl.when(block + 1 < blocks)
        def _():
            for copy in fetch(amplitude, slab, sems, 1 - slot, first_atom + owned, owned):
                copy.start()

        left = jnp.concatenate(
            [slab.at[slot, piece].reshape(rows, LANES)[...] for piece in range(pieces)], axis=1
        )
        mine = partial.at[pl.ds(first_atom, owned)]
        for number, (first, width) in enumerate(chunks):
            product = jnp.dot(
                left, ps_form[:, pl.ds(first, width)], preferred_element_type=jnp.float32
            )
            acc = accs[number % 2]
            for tile in range(width // LANES):
                acc[tile] = product[:, tile * LANES : (tile + 1) * LANES]
            if number:
                weigh(
                    accs[1 - number % 2], weights, levels, mine, first_atom, chunks[number - 1], sizes
                )
        weigh(
            accs[(len(chunks) - 1) % 2], weights, levels, mine, first_atom, chunks[-1], sizes
        )
        return carry

    lax.fori_loop(0, blocks, step, 0)


def point_weights(sixj, projector, l_ps, qinverse):
    level_count = sixj.shape[2]
    onehot_ps = (l_ps[:, None] == jnp.arange(level_count, dtype=jnp.int32)).astype(jnp.float32)
    points = jnp.einsum("jlxy,lg->xjgy", sixj, projector, precision=lax.Precision.HIGHEST)
    widened = jnp.repeat(onehot_ps, qinverse.shape[2] // l_ps.shape[0], axis=0)
    spread = jnp.einsum("xjgy,cy->xjgc", points, widened, precision=lax.Precision.HIGHEST)
    value = spread[:, :, None] * jnp.transpose(qinverse, (1, 0, 2))[None, None]
    return value.reshape(level_count, -1, *value.shape[3:])


def local(amplitude, ps_form, kgrid, l_atom, l_ps, sixj):
    if amplitude.shape[2] != 2 or amplitude.shape[2] * sixj.shape[0] != 8:
        return plain(amplitude, ps_form, kgrid, l_atom, l_ps, sixj)
    grid_count, channels, slab_points, radial = amplitude.shape
    columns = ps_form.shape[1]
    kpoints = kgrid.shape[0]
    ps_channels = columns // kpoints
    degrees = sixj.shape[1]
    ang_size = lax.axis_size("ang")
    owned = channels // ang_size
    grid_nodes, projector = legendre_table(
        lax.axis_index("ang") * grid_count, grid_count, grid_count * ang_size, degrees
    )
    krow = lax.dynamic_slice_in_dim(kgrid, lax.axis_index("kslab") * slab_points, slab_points)[
        None, :, None
    ]
    kcol = jnp.tile(kgrid, ps_channels)[None, None, :]
    qinverse = 1.0 / (
        1.0 + krow * krow + kcol * kcol - 2.0 * grid_nodes[:, None, None] * krow * kcol
    )
    total_j = sixj.shape[0]
    sizes = (grid_count, owned, slab_points, total_j)
    rows = grid_count * owned * slab_points
    pieces = radial // LANES
    partial = pl.pallas_call(
        functools.partial(block_kernel, sizes),
        out_shape=jax.ShapeDtypeStruct((channels, total_j * slab_points, columns), jnp.float32),
        in_specs=[
            pl.BlockSpec(memory_space=pl.ANY),
            pl.BlockSpec(memory_space=pltpu.VMEM),
            pl.BlockSpec(memory_space=pltpu.VMEM),
            pl.BlockSpec(memory_space=pltpu.SMEM),
        ],
        out_specs=pl.BlockSpec(memory_space=pltpu.VMEM),
        scratch_shapes=[
            pltpu.VMEM((2, pieces, grid_count, owned, slab_points, LANES), jnp.bfloat16),
            pltpu.VMEM((2, rows, LANES), jnp.float32),
            pltpu.VMEM((2, rows, LANES), jnp.float32),
            pltpu.SemaphoreType.DMA((2, pieces)),
        ],
        compiler_params=pltpu.CompilerParams(vmem_limit_bytes=56 << 20),
        name="block_kernel",
    )(amplitude, ps_form, point_weights(sixj, projector, l_ps, qinverse), l_atom)
    summed = lax.psum_scatter(partial, "ang", scatter_dimension=0, tiled=True)
    summed = summed.reshape(owned, total_j, slab_points, columns)
    return lax.all_to_all(summed, "kslab", split_axis=1, concat_axis=2, tiled=True)


def solution(mesh):
    in_specs = (P("ang", None, "kslab", None), P(), P(), P(), P(), P())
    out_specs = P("ang", "kslab", None, None)
    return jax.shard_map(local, mesh=mesh, in_specs=in_specs, out_specs=out_specs, check_vma=False)
```

```python
import functools

import jax
import jax.numpy as jnp
from jax import lax
from jax.experimental import pallas as pl
from jax.experimental.pallas import tpu as pltpu
from jax.sharding import PartitionSpec as P


def legendre_table(first_row, row_count, total_points, degrees):
    positions = (first_row + jnp.arange(row_count)).astype(jnp.float32)
    angles = jnp.pi * (positions + 0.5) / total_points
    grid_nodes = jnp.cos(angles)
    grid_weights = jnp.pi / total_points * jnp.sin(angles)
    series = [jnp.ones_like(grid_nodes), grid_nodes]
    for degree in range(1, degrees - 1):
        series.append(
            ((2 * degree + 1) * grid_nodes * series[-1] - degree * series[-2]) / (degree + 1)
        )
    return (grid_nodes, grid_weights[None, :] * jnp.stack(series[:degrees]))


def recouple(values, l_atom, l_ps, sixj, kpoints):
    levels = jnp.arange(sixj.shape[2], dtype=jnp.int32)
    onehot_atom = (l_atom[:, None] == levels[None, :]).astype(jnp.float32)
    onehot_ps = (l_ps[:, None] == levels[None, :]).astype(jnp.float32)
    coupling = jnp.einsum(
        "jlxy,ax,by->ajlb", sixj, onehot_atom, onehot_ps, precision=lax.Precision.HIGHEST
    )
    widened = jnp.repeat(coupling, kpoints, axis=3)
    return jnp.einsum("ajlc,alkc->ajkc", widened, values, precision=lax.Precision.HIGHEST)


def plain(amplitude, ps_form, kgrid, l_atom, l_ps, sixj):
    grid_count, channels, slab_points, radial = amplitude.shape
    columns = ps_form.shape[1]
    kpoints = kgrid.shape[0]
    ps_channels = columns // kpoints
    degrees = sixj.shape[1]
    ang_size = lax.axis_size("ang")
    owned = channels // ang_size
    grid_nodes, projector = legendre_table(
        lax.axis_index("ang") * grid_count, grid_count, grid_count * ang_size, degrees
    )
    krow = lax.dynamic_slice_in_dim(kgrid, lax.axis_index("kslab") * slab_points, slab_points)[
        None, :, None
    ]
    kcol = jnp.tile(kgrid, ps_channels)[None, None, :]
    qinverse = 1.0 / (
        1.0 + krow * krow + kcol * kcol - 2.0 * grid_nodes[:, None, None] * krow * kcol
    )
    intersection = jnp.dot(
        amplitude.reshape(-1, radial), ps_form, preferred_element_type=jnp.float32
    )
    intersection = intersection.reshape(
        grid_count, lax.axis_size("ang") * owned, slab_points, columns
    )
    integrand = intersection * qinverse[:, None]
    partial = jnp.einsum("lg,gakc->alkc", projector, integrand, precision=lax.Precision.HIGHEST)
    partial = recouple(partial, l_atom, l_ps, sixj, kpoints)
    summed = lax.psum_scatter(partial, "ang", scatter_dimension=0, tiled=True)
    return lax.all_to_all(summed, "kslab", split_axis=1, concat_axis=2, tiled=True)


LANES = 128
HALVES = 2


def column_chunks(columns):
    width = LANES * (-(-columns // (2 * LANES)))
    return [(0, width), (width, columns - width)]


def weigh(acc, weights, levels, partial, first_atom, chunk, sizes):
    grid_count, owned, slab_points, total_j = sizes
    first, width = chunk
    group = owned * slab_points
    for atom in range(owned):
        level = levels[first_atom + atom]
        for tile in range(width // LANES):
            lanes = pl.ds(first + tile * LANES, LANES)
            points = [
                acc[tile, pl.ds(atom * slab_points + k, grid_count, stride=group), :]
                for k in range(slab_points)
            ]
            rows = []
            for j in range(total_j):
                for k in range(slab_points):
                    term = points[k] * weights[level, j * slab_points + k, :, lanes]
                    rows.append(jnp.sum(term, axis=0, keepdims=True))
            partial[atom, :, lanes] = jnp.concatenate(rows, axis=0)


def fetch(amplitude, slab, sems, slot, first_atom, owned):
    return [
        pltpu.make_async_copy(
            amplitude.at[:, pl.ds(first_atom, owned), :, pl.ds(piece * LANES, LANES)],
            slab.at[slot, piece],
            sems.at[slot, piece],
        )
        for piece in range(slab.shape[1])
    ]


def block_kernel(
    sizes,
    amplitude,
    ps_source,
    points,
    ps_levels,
    kgrid,
    levels,
    out,
    ps_form,
    onehot,
    qinverse,
    slab,
    acc_a,
    acc_b,
    weights,
    parts,
    core_in,
    chip_in,
    slices,
    slices_in,
    sems,
    core_sems,
    chip_sems,
    slab_sems,
    ps_sem,
):
    grid_count, owned, slab_points, total_j = sizes
    pieces = slab.shape[1]
    rows = grid_count * owned * slab_points
    blocks = 2 * chip_in.shape[1] + 2
    halves = parts.shape[0] // blocks
    chips = blocks // 2
    last_acc = (acc_a, acc_b)[1]
    kpoints = kgrid.shape[0]
    columns = ps_form.shape[1]
    chunks = column_chunks(ps_form.shape[1])
    accs = (acc_a, acc_b)
    me = lax.axis_index("ang")
    z = lax.axis_index("kslab")
    core = lax.rem(me, 2)
    chip_x = lax.rem(me // 2, 2)
    chip_y = me // 4
    other_core = me + 1 - 2 * core

    def chip_at(turn):
        x = lax.rem(chip_x + 1 - turn // 2, 2)
        y = lax.rem(chip_y + lax.rem(turn + 1, 2), 2)
        return 2 * y + x

    def first_of(unit):
        half, block = unit // blocks, lax.rem(unit, blocks)
        owner = 2 * chip_at(block // 2) + lax.rem(core + 1 + lax.rem(block, 2), 2)
        return (owner * halves + half) * owned

    def to_core(half, turn):
        return pltpu.make_async_remote_copy(
            src_ref=parts.at[half * blocks + 2 * turn],
            dst_ref=core_in.at[half, turn],
            send_sem=core_sems.at[0, half, turn],
            recv_sem=core_sems.at[1, half, turn],
            device_id={"ang": other_core},
            device_id_type=pl.DeviceIdType.MESH,
        )

    def to_chip(half, turn):
        return pltpu.make_async_remote_copy(
            src_ref=parts.at[half * blocks + 2 * turn + 1],
            dst_ref=chip_in.at[half, turn],
            send_sem=chip_sems.at[0, half, turn],
            recv_sem=chip_sems.at[1, half, turn],
            device_id={"ang": 2 * chip_at(turn) + core},
            device_id_type=pl.DeviceIdType.MESH,
        )

    def to_slab(half, away):
        target = lax.rem(z + away, total_j)
        return pltpu.make_async_remote_copy(
            src_ref=slices.at[half, target],
            dst_ref=slices_in.at[half, z],
            send_sem=slab_sems.at[0, half, away],
            recv_sem=slab_sems.at[1, half, away],
            device_id={"kslab": target},
            device_id_type=pl.DeviceIdType.MESH,
        )

    for copy in fetch(amplitude, slab, sems, 0, first_of(0), owned):
        copy.start()
    ps_copy = pltpu.make_async_copy(ps_source, ps_form, ps_sem)
    ps_copy.start()
    barrier = pltpu.get_barrier_semaphore()
    greeted = [{"ang": other_core}]
    greeted += [{"ang": 2 * chip_at(turn) + core} for turn in range(chips - 1)]
    greeted += [{"kslab": lax.rem(z + away, total_j)} for away in range(1, total_j)]
    for device in greeted:
        pl.semaphore_signal(
            barrier, inc=1, device_id=device, device_id_type=pl.DeviceIdType.MESH
        )
    pl.semaphore_wait(barrier, len(greeted))

    member = lax.broadcasted_iota(jnp.int32, (ps_levels.shape[1], columns), 1) - (
        kpoints * lax.broadcasted_iota(jnp.int32, (ps_levels.shape[1], columns), 0)
    )
    member = jnp.where((member >= 0) & (member < kpoints), 1.0, 0.0).astype(jnp.bfloat16)
    level_rows = lax.broadcasted_iota(jnp.int32, (weights.shape[0], ps_levels.shape[1]), 0)
    known = jnp.where(level_rows == ps_levels[...], 1.0, 0.0).astype(jnp.bfloat16)
    onehot[...] = jnp.dot(known, member, preferred_element_type=jnp.float32)

    tile_shape = (grid_count, LANES)
    place = me * grid_count + lax.broadcasted_iota(jnp.int32, tile_shape, 0)
    total_points = grid_count * blocks
    nodes = jnp.cos(jnp.pi * (place.astype(jnp.float32) + 0.5) / total_points)
    kindex = lax.broadcasted_iota(jnp.int32, tile_shape, 1) & (kpoints - 1)
    kcol = jnp.zeros(tile_shape, jnp.float32)
    for q in range(kpoints):
        kcol = jnp.where(kindex == q, kgrid[q], kcol)
    for k in range(slab_points):
        krow = kgrid[z * slab_points + k]
        value = 1.0 / (1.0 + krow * krow + kcol * kcol - 2.0 * nodes * krow * kcol)
        for tile in range(columns // LANES):
            qinverse[k, :, tile * LANES : (tile + 1) * LANES] = value

    def weight_level(level, carry):
        spread = jnp.dot(
            points[level],
            onehot[...],
            precision=lax.Precision.HIGHEST,
            preferred_element_type=jnp.float32,
        )
        for j in range(total_j):
            for k in range(slab_points):
                weights[level, j * slab_points + k] = (
                    spread[j * grid_count : (j + 1) * grid_count] * qinverse[k]
                )
        return carry

    lax.fori_loop(0, weights.shape[0], weight_level, 0)
    last_acc[...] = jnp.zeros_like(last_acc)
    ps_copy.wait()

    def multiply(slot, number):
        first, width = chunks[number]
        left = jnp.concatenate(
            [slab.at[slot, piece].reshape(rows, LANES)[...] for piece in range(pieces)], axis=1
        )
        product = jnp.dot(
            left, ps_form[:, pl.ds(first, width)], preferred_element_type=jnp.float32
        )
        for tile in range(width // LANES):
            accs[number][tile] = product[:, tile * LANES : (tile + 1) * LANES]

    def weigh_unit(unit, number):
        weigh(
            accs[number], weights, levels, parts.at[unit], first_of(unit), chunks[number], sizes
        )

    def finish(unit):
        half, block = unit // blocks, lax.rem(unit, blocks)
        turn = block // 2

        @pl.when(lax.rem(block, 2) == 0)
        def _():
            to_core(half, turn).start()

        @pl.when(lax.rem(block, 2) == 1)
        def _():
            to_core(half, turn).wait_recv()

            @pl.when(turn < chips - 1)
            def _():
                parts[unit] = parts[unit] + core_in[half, turn]
                to_chip(half, turn).start()

            @pl.when(turn == chips - 1)
            def _():
                for earlier in range(chips - 1):
                    to_chip(half, earlier).wait_recv()

                def total_atom(atom, carry):
                    total = parts[unit, atom] + core_in[half, chips - 1, atom]
                    for earlier in range(chips - 1):
                        total = total + chip_in[half, earlier, atom]
                    for j in range(total_j):
                        slices[half, j, atom] = total[j * slab_points : (j + 1) * slab_points]
                    return carry

                lax.fori_loop(0, owned, total_atom, 0)
                for away in range(1, total_j):
                    to_slab(half, away).start()
                slices_in[half, z] = slices[half, z]

    def step(unit, carry):
        slot = lax.rem(unit, 2)
        for copy in fetch(amplitude, slab, sems, slot, first_of(unit), owned):
            copy.wait()

        @pl.when(unit + 1 < halves * blocks)
        def _():
            for copy in fetch(amplitude, slab, sems, 1 - slot, first_of(unit + 1), owned):
                copy.start()

        multiply(slot, 0)
        weigh_unit(jnp.maximum(unit - 1, 0), 1)

        @pl.when(unit > 0)
        def _():
            finish(unit - 1)

        multiply(slot, 1)
        weigh_unit(unit, 0)
        return carry

    units = halves * blocks
    lax.fori_loop(0, units, step, 0)
    weigh_unit(units - 1, 1)
    finish(units - 1)

    for half in range(halves):
        for away in range(1, total_j):
            to_slab(half, away).wait_recv()

        def place_atom(atom, carry):
            out[half * owned + atom, 0] = jnp.concatenate(
                [slices_in[half, j, atom] for j in range(total_j)], axis=0
            )
            return carry

        lax.fori_loop(0, owned, place_atom, 0)
    for half in range(halves):
        for turn in range(chips):
            to_core(half, turn).wait_send()
        for turn in range(chips - 1):
            to_chip(half, turn).wait_send()
        for away in range(1, total_j):
            to_slab(half, away).wait_send()


def point_weights(sixj, projector):
    points = jnp.einsum("jlxy,lg->xjgy", sixj, projector, precision=lax.Precision.HIGHEST)
    return points.reshape(sixj.shape[2], -1, sixj.shape[3])


def local(amplitude, ps_form, kgrid, l_atom, l_ps, sixj):
    if (amplitude.shape[2], sixj.shape[0], lax.axis_size("ang"), lax.axis_size("kslab")) != (2, 4, 8, 4):
        return plain(amplitude, ps_form, kgrid, l_atom, l_ps, sixj)
    grid_count, channels, slab_points, radial = amplitude.shape
    columns = ps_form.shape[1]
    kpoints = kgrid.shape[0]
    ps_channels = columns // kpoints
    degrees = sixj.shape[1]
    ang_size = lax.axis_size("ang")
    owned = channels // ang_size
    grid_nodes, projector = legendre_table(
        lax.axis_index("ang") * grid_count, grid_count, grid_count * ang_size, degrees
    )
    total_j = sixj.shape[0]
    halves = HALVES if owned % HALVES == 0 else 1
    share = owned // halves
    sizes = (grid_count, share, slab_points, total_j)
    rows = grid_count * share * slab_points
    wide = column_chunks(columns)
    pieces = radial // LANES
    level_count = sixj.shape[2]
    parts_shape = (share, total_j * slab_points, columns)
    slice_shape = (halves, total_j, share, slab_points, columns)
    chips = ang_size // 2
    in_vmem = pl.BlockSpec(memory_space=pltpu.VMEM)
    return pl.pallas_call(
        functools.partial(block_kernel, sizes),
        out_shape=jax.ShapeDtypeStruct((owned, 1, kpoints, columns), jnp.float32),
        in_specs=[pl.BlockSpec(memory_space=pl.ANY)] * 2
        + [in_vmem] * 2
        + [pl.BlockSpec(memory_space=pltpu.SMEM)] * 2,
        out_specs=in_vmem,
        scratch_shapes=[
            pltpu.VMEM((radial, columns), jnp.bfloat16),
            pltpu.VMEM((level_count, columns), jnp.float32),
            pltpu.VMEM((slab_points, grid_count, columns), jnp.float32),
            pltpu.VMEM((2, pieces, grid_count, share, slab_points, LANES), jnp.bfloat16),
            pltpu.VMEM((wide[0][1] // LANES, rows, LANES), jnp.float32),
            pltpu.VMEM((wide[1][1] // LANES, rows, LANES), jnp.float32),
            pltpu.VMEM((level_count, total_j * slab_points, grid_count, columns), jnp.float32),
            pltpu.VMEM((halves * ang_size,) + parts_shape, jnp.float32),
            pltpu.VMEM((halves, chips) + parts_shape, jnp.float32),
            pltpu.VMEM((halves, chips - 1) + parts_shape, jnp.float32),
            pltpu.VMEM(slice_shape, jnp.float32),
            pltpu.VMEM(slice_shape, jnp.float32),
            pltpu.SemaphoreType.DMA((2, pieces)),
            pltpu.SemaphoreType.DMA((2, halves, chips)),
            pltpu.SemaphoreType.DMA((2, halves, chips)),
            pltpu.SemaphoreType.DMA((2, halves, total_j)),
            pltpu.SemaphoreType.DMA,
        ],
        compiler_params=pltpu.CompilerParams(
            vmem_limit_bytes=56 << 20, collective_id=0, has_side_effects=True
        ),
        name="block_kernel",
    )(
        amplitude,
        ps_form,
        point_weights(sixj, projector),
        l_ps.reshape(1, ps_channels),
        kgrid,
        l_atom,
    )


def solution(mesh):
    in_specs = (P("ang", None, "kslab", None), P(), P(), P(), P(), P())
    out_specs = P("ang", "kslab", None, None)
    return jax.shard_map(local, mesh=mesh, in_specs=in_specs, out_specs=out_specs, check_vma=False)
```

```python
import functools

import jax
import jax.numpy as jnp
from jax import lax
from jax.experimental import pallas as pl
from jax.experimental.pallas import tpu as pltpu
from jax.sharding import PartitionSpec as P


def legendre_table(first_row, row_count, total_points, degrees):
    positions = (first_row + jnp.arange(row_count)).astype(jnp.float32)
    angles = jnp.pi * (positions + 0.5) / total_points
    grid_nodes = jnp.cos(angles)
    grid_weights = jnp.pi / total_points * jnp.sin(angles)
    series = [jnp.ones_like(grid_nodes), grid_nodes]
    for degree in range(1, degrees - 1):
        series.append(
            ((2 * degree + 1) * grid_nodes * series[-1] - degree * series[-2]) / (degree + 1)
        )
    return (grid_nodes, grid_weights[None, :] * jnp.stack(series[:degrees]))


def recouple(values, l_atom, l_ps, sixj, kpoints):
    levels = jnp.arange(sixj.shape[2], dtype=jnp.int32)
    onehot_atom = (l_atom[:, None] == levels[None, :]).astype(jnp.float32)
    onehot_ps = (l_ps[:, None] == levels[None, :]).astype(jnp.float32)
    coupling = jnp.einsum(
        "jlxy,ax,by->ajlb", sixj, onehot_atom, onehot_ps, precision=lax.Precision.HIGHEST
    )
    widened = jnp.repeat(coupling, kpoints, axis=3)
    return jnp.einsum("ajlc,alkc->ajkc", widened, values, precision=lax.Precision.HIGHEST)


def plain(amplitude, ps_form, kgrid, l_atom, l_ps, sixj):
    grid_count, channels, slab_points, radial = amplitude.shape
    columns = ps_form.shape[1]
    kpoints = kgrid.shape[0]
    ps_channels = columns // kpoints
    degrees = sixj.shape[1]
    ang_size = lax.axis_size("ang")
    owned = channels // ang_size
    grid_nodes, projector = legendre_table(
        lax.axis_index("ang") * grid_count, grid_count, grid_count * ang_size, degrees
    )
    krow = lax.dynamic_slice_in_dim(kgrid, lax.axis_index("kslab") * slab_points, slab_points)[
        None, :, None
    ]
    kcol = jnp.tile(kgrid, ps_channels)[None, None, :]
    qinverse = 1.0 / (
        1.0 + krow * krow + kcol * kcol - 2.0 * grid_nodes[:, None, None] * krow * kcol
    )
    intersection = jnp.dot(
        amplitude.reshape(-1, radial), ps_form, preferred_element_type=jnp.float32
    )
    intersection = intersection.reshape(
        grid_count, lax.axis_size("ang") * owned, slab_points, columns
    )
    integrand = intersection * qinverse[:, None]
    partial = jnp.einsum("lg,gakc->alkc", projector, integrand, precision=lax.Precision.HIGHEST)
    partial = recouple(partial, l_atom, l_ps, sixj, kpoints)
    summed = lax.psum_scatter(partial, "ang", scatter_dimension=0, tiled=True)
    return lax.all_to_all(summed, "kslab", split_axis=1, concat_axis=2, tiled=True)


LANES = 128
HALVES = 2
SLOTS = 6


def column_chunks(columns):
    width = LANES * (-(-columns // (2 * LANES)))
    return [(0, width), (width, columns - width)]


def weigh(acc, weights, levels, partial, first_atom, chunk, sizes):
    grid_count, owned, slab_points, total_j = sizes
    first, width = chunk
    group = owned * slab_points
    for atom in range(owned):
        level = levels[first_atom + atom]
        for tile in range(width // LANES):
            lanes = pl.ds(first + tile * LANES, LANES)
            points = [
                acc[tile, pl.ds(atom * slab_points + k, grid_count, stride=group), :]
                for k in range(slab_points)
            ]
            rows = []
            for j in range(total_j):
                for k in range(slab_points):
                    term = points[k] * weights[level, j * slab_points + k, :, lanes]
                    rows.append(jnp.sum(term, axis=0, keepdims=True))
            partial[atom, :, lanes] = jnp.concatenate(rows, axis=0)


def fetch(amplitude, slab, sems, slot, first_atom, owned):
    return [
        pltpu.make_async_copy(
            amplitude.at[:, pl.ds(first_atom, owned), :, pl.ds(piece * LANES, LANES)],
            slab.at[slot, piece],
            sems.at[slot, piece],
        )
        for piece in range(slab.shape[1])
    ]


def block_kernel(
    sizes,
    amplitude,
    ps_source,
    points,
    ps_levels,
    kgrid,
    levels,
    out,
    ps_form,
    onehot,
    qinverse,
    slab,
    acc_a,
    acc_b,
    weights,
    parts,
    core_in,
    chip_in,
    slices,
    slices_in,
    sems,
    core_sems,
    chip_sems,
    slab_sems,
    ps_sem,
):
    grid_count, owned, slab_points, total_j = sizes
    pieces = slab.shape[1]
    rows = grid_count * owned * slab_points
    blocks = 2 * chip_in.shape[1] + 2
    halves = parts.shape[0] // blocks
    chips = blocks // 2
    last_acc = (acc_a, acc_b)[1]
    kpoints = kgrid.shape[0]
    columns = ps_form.shape[1]
    chunks = column_chunks(ps_form.shape[1])
    accs = (acc_a, acc_b)
    me = lax.axis_index("ang")
    z = lax.axis_index("kslab")
    core = lax.rem(me, 2)
    chip_x = lax.rem(me // 2, 2)
    chip_y = me // 4
    other_core = me + 1 - 2 * core

    def chip_at(turn):
        x = lax.rem(chip_x + 1 - turn // 2, 2)
        y = lax.rem(chip_y + lax.rem(turn + 1, 2), 2)
        return 2 * y + x

    def first_of(unit):
        half, block = unit // blocks, lax.rem(unit, blocks)
        owner = 2 * chip_at(block // 2) + lax.rem(core + 1 + lax.rem(block, 2), 2)
        return (owner * halves + half) * owned

    def to_core(half, turn):
        return pltpu.make_async_remote_copy(
            src_ref=parts.at[half * blocks + 2 * turn],
            dst_ref=core_in.at[half, turn],
            send_sem=core_sems.at[0, half, turn],
            recv_sem=core_sems.at[1, half, turn],
            device_id={"ang": other_core},
            device_id_type=pl.DeviceIdType.MESH,
        )

    def to_chip(half, turn):
        return pltpu.make_async_remote_copy(
            src_ref=parts.at[half * blocks + 2 * turn + 1],
            dst_ref=chip_in.at[half, turn],
            send_sem=chip_sems.at[0, half, turn],
            recv_sem=chip_sems.at[1, half, turn],
            device_id={"ang": 2 * chip_at(turn) + core},
            device_id_type=pl.DeviceIdType.MESH,
        )

    def to_slab(half, away):
        target = lax.rem(z + away, total_j)
        return pltpu.make_async_remote_copy(
            src_ref=slices.at[half, target],
            dst_ref=slices_in.at[half, z],
            send_sem=slab_sems.at[0, half, away],
            recv_sem=slab_sems.at[1, half, away],
            device_id={"kslab": target},
            device_id_type=pl.DeviceIdType.MESH,
        )

    units = halves * blocks
    slots = slab.shape[0]

    def start_fetch(unit):
        for copy in fetch(amplitude, slab, sems, lax.rem(unit, slots), first_of(unit), owned):
            copy.start()

    start_fetch(0)
    ps_copy = pltpu.make_async_copy(ps_source, ps_form, ps_sem)
    ps_copy.start()
    barrier = pltpu.get_barrier_semaphore()
    greeted = [{"ang": other_core}]
    greeted += [{"ang": 2 * chip_at(turn) + core} for turn in range(chips - 1)]
    greeted += [{"kslab": lax.rem(z + away, total_j)} for away in range(1, total_j)]
    for device in greeted:
        pl.semaphore_signal(
            barrier, inc=1, device_id=device, device_id_type=pl.DeviceIdType.MESH
        )
    def start_early(unit, carry):
        start_fetch(unit)
        return carry

    lax.fori_loop(1, min(slots - 1, units), start_early, 0)

    member = lax.broadcasted_iota(jnp.int32, (ps_levels.shape[1], columns), 1) - (
        kpoints * lax.broadcasted_iota(jnp.int32, (ps_levels.shape[1], columns), 0)
    )
    member = jnp.where((member >= 0) & (member < kpoints), 1.0, 0.0).astype(jnp.bfloat16)
    level_rows = lax.broadcasted_iota(jnp.int32, (weights.shape[0], ps_levels.shape[1]), 0)
    known = jnp.where(level_rows == ps_levels[...], 1.0, 0.0).astype(jnp.bfloat16)
    spread_rows = jnp.dot(known, member, preferred_element_type=jnp.float32)
    onehot[...] = jnp.concatenate([spread_rows] * 3, axis=0).astype(jnp.bfloat16)

    tile_shape = (grid_count, LANES)
    place = me * grid_count + lax.broadcasted_iota(jnp.int32, tile_shape, 0)
    total_points = grid_count * blocks
    nodes = jnp.cos(jnp.pi * (place.astype(jnp.float32) + 0.5) / total_points)
    kindex = lax.broadcasted_iota(jnp.int32, tile_shape, 1) & (kpoints - 1)
    kcol = jnp.zeros(tile_shape, jnp.float32)
    for q in range(kpoints):
        kcol = jnp.where(kindex == q, kgrid[q], kcol)
    for k in range(slab_points):
        krow = kgrid[z * slab_points + k]
        value = 1.0 / (1.0 + krow * krow + kcol * kcol - 2.0 * nodes * krow * kcol)
        for tile in range(columns // LANES):
            qinverse[k, :, tile * LANES : (tile + 1) * LANES] = value

    group = 4
    level_size = total_j * grid_count
    for first_level in range(0, weights.shape[0], group):
        whole = points[first_level : first_level + group].reshape(group * level_size, -1)
        high = whole.astype(jnp.bfloat16).astype(jnp.float32)
        middle = (whole - high).astype(jnp.bfloat16).astype(jnp.float32)
        low = whole - high - middle
        spread = jnp.dot(
            jnp.concatenate([high, middle, low], axis=1).astype(jnp.bfloat16),
            onehot[...],
            preferred_element_type=jnp.float32,
        )
        for part in range(group * total_j):
            rows_of = spread[part * grid_count : (part + 1) * grid_count]
            for k in range(slab_points):
                weights[first_level + part // total_j, part % total_j * slab_points + k] = (
                    rows_of * qinverse[k]
                )
    pl.semaphore_wait(barrier, len(greeted))
    last_acc[...] = jnp.zeros_like(last_acc)
    ps_copy.wait()

    def multiply(slot, number):
        first, width = chunks[number]
        left = jnp.concatenate(
            [slab.at[slot, piece].reshape(rows, LANES)[...] for piece in range(pieces)], axis=1
        )
        product = jnp.dot(
            left, ps_form[:, pl.ds(first, width)], preferred_element_type=jnp.float32
        )
        for tile in range(width // LANES):
            accs[number][tile] = product[:, tile * LANES : (tile + 1) * LANES]

    def weigh_unit(unit, number):
        weigh(
            accs[number], weights, levels, parts.at[unit], first_of(unit), chunks[number], sizes
        )

    def finish(unit):
        half, block = unit // blocks, lax.rem(unit, blocks)
        turn = block // 2

        @pl.when(lax.rem(block, 2) == 0)
        def _():
            to_core(half, turn).start()

        @pl.when(lax.rem(block, 2) == 1)
        def _():
            to_core(half, turn).wait_recv()

            @pl.when(turn < chips - 1)
            def _():
                parts[unit] = parts[unit] + core_in[half, turn]
                to_chip(half, turn).start()

            @pl.when(turn == chips - 1)
            def _():
                for earlier in range(chips - 1):
                    to_chip(half, earlier).wait_recv()

                def total_atom(atom, carry):
                    total = parts[unit, atom] + core_in[half, chips - 1, atom]
                    for earlier in range(chips - 1):
                        total = total + chip_in[half, earlier, atom]
                    for j in range(total_j):
                        slices[half, j, atom] = total[j * slab_points : (j + 1) * slab_points]
                    return carry

                lax.fori_loop(0, owned, total_atom, 0)
                for away in range(1, total_j):
                    to_slab(half, away).start()
                slices_in[half, z] = slices[half, z]

    def step(unit, carry):
        slot = lax.rem(unit, slots)
        for copy in fetch(amplitude, slab, sems, slot, first_of(unit), owned):
            copy.wait()

        @pl.when(unit + slots - 1 < units)
        def _():
            start_fetch(unit + slots - 1)

        multiply(slot, 0)
        weigh_unit(jnp.maximum(unit - 1, 0), 1)

        @pl.when(unit > 0)
        def _():
            finish(unit - 1)

        multiply(slot, 1)
        weigh_unit(unit, 0)
        return carry

    lax.fori_loop(0, units, step, 0)
    weigh_unit(units - 1, 1)
    finish(units - 1)

    for half in range(halves):
        for away in range(1, total_j):
            to_slab(half, away).wait_recv()

        def place_atom(atom, carry):
            out[half * owned + atom, 0] = jnp.concatenate(
                [slices_in[half, j, atom] for j in range(total_j)], axis=0
            )
            return carry

        lax.fori_loop(0, owned, place_atom, 0)
    for half in range(halves):
        for turn in range(chips):
            to_core(half, turn).wait_send()
        for turn in range(chips - 1):
            to_chip(half, turn).wait_send()
        for away in range(1, total_j):
            to_slab(half, away).wait_send()


def point_weights(sixj, projector):
    points = jnp.einsum("jlxy,lg->xjgy", sixj, projector, precision=lax.Precision.HIGHEST)
    return points.reshape(sixj.shape[2], -1, sixj.shape[3])


def local(amplitude, ps_form, kgrid, l_atom, l_ps, sixj):
    if (amplitude.shape[2], sixj.shape[0], lax.axis_size("ang"), lax.axis_size("kslab")) != (2, 4, 8, 4):
        return plain(amplitude, ps_form, kgrid, l_atom, l_ps, sixj)
    grid_count, channels, slab_points, radial = amplitude.shape
    columns = ps_form.shape[1]
    kpoints = kgrid.shape[0]
    ps_channels = columns // kpoints
    degrees = sixj.shape[1]
    ang_size = lax.axis_size("ang")
    owned = channels // ang_size
    grid_nodes, projector = legendre_table(
        lax.axis_index("ang") * grid_count, grid_count, grid_count * ang_size, degrees
    )
    total_j = sixj.shape[0]
    halves = HALVES if owned % HALVES == 0 else 1
    share = owned // halves
    sizes = (grid_count, share, slab_points, total_j)
    rows = grid_count * share * slab_points
    wide = column_chunks(columns)
    pieces = radial // LANES
    level_count = sixj.shape[2]
    parts_shape = (share, total_j * slab_points, columns)
    slice_shape = (halves, total_j, share, slab_points, columns)
    chips = ang_size // 2
    in_vmem = pl.BlockSpec(memory_space=pltpu.VMEM)
    return pl.pallas_call(
        functools.partial(block_kernel, sizes),
        out_shape=jax.ShapeDtypeStruct((owned, 1, kpoints, columns), jnp.float32),
        in_specs=[pl.BlockSpec(memory_space=pl.ANY)] * 2
        + [in_vmem] * 2
        + [pl.BlockSpec(memory_space=pltpu.SMEM)] * 2,
        out_specs=in_vmem,
        scratch_shapes=[
            pltpu.VMEM((radial, columns), jnp.bfloat16),
            pltpu.VMEM((3 * level_count, columns), jnp.bfloat16),
            pltpu.VMEM((slab_points, grid_count, columns), jnp.float32),
            pltpu.VMEM((SLOTS, pieces, grid_count, share, slab_points, LANES), jnp.bfloat16),
            pltpu.VMEM((wide[0][1] // LANES, rows, LANES), jnp.float32),
            pltpu.VMEM((wide[1][1] // LANES, rows, LANES), jnp.float32),
            pltpu.VMEM((level_count, total_j * slab_points, grid_count, columns), jnp.float32),
            pltpu.VMEM((halves * ang_size,) + parts_shape, jnp.float32),
            pltpu.VMEM((halves, chips) + parts_shape, jnp.float32),
            pltpu.VMEM((halves, chips - 1) + parts_shape, jnp.float32),
            pltpu.VMEM(slice_shape, jnp.float32),
            pltpu.VMEM(slice_shape, jnp.float32),
            pltpu.SemaphoreType.DMA((SLOTS, pieces)),
            pltpu.SemaphoreType.DMA((2, halves, chips)),
            pltpu.SemaphoreType.DMA((2, halves, chips)),
            pltpu.SemaphoreType.DMA((2, halves, total_j)),
            pltpu.SemaphoreType.DMA,
        ],
        compiler_params=pltpu.CompilerParams(
            vmem_limit_bytes=56 << 20, collective_id=0, has_side_effects=True
        ),
        name="block_kernel",
    )(
        amplitude,
        ps_form,
        point_weights(sixj, projector),
        l_ps.reshape(1, ps_channels),
        kgrid,
        l_atom,
    )


def solution(mesh):
    in_specs = (P("ang", None, "kslab", None), P(), P(), P(), P(), P())
    out_specs = P("ang", "kslab", None, None)
    return jax.shard_map(local, mesh=mesh, in_specs=in_specs, out_specs=out_specs, check_vma=False)
```
